512 devices in a mesh: patch: 64 (over y_lo, z, core), tensor: 8 (over x, y_hi).
Axes of the slice: x: 4, y: 8 (y_hi: 2, y_lo: 4; y = y_hi * 4 + y_lo), z: 8, core: 2. Of those that a mesh axis runs over, the one named last changes fastest.
Arguments:
- hidden_in: bfloat16 [8192, 5120], P('patch', 'tensor'), may hold values from -6 to 6
- queries: bfloat16 [8192, 3072], P('patch', 'tensor'), may hold values from -16 to 16
- fresh_keys: bfloat16 [8192, 3072], P('patch', 'tensor'), may hold values from -6 to 6
- fresh_values: bfloat16 [8192, 3072], P('patch', 'tensor'), may hold values from -6 to 6
- stale_keys: bfloat16 [8192, 3072], P('patch', 'tensor'), may hold values from -8 to 8
- stale_values: bfloat16 [8192, 3072], P('patch', 'tensor'), may hold values from -6 to 6
- out_weight: bfloat16 [3072, 5120], P('tensor'), may hold values from -0.5 to 0.5
- gate: float32 [5120], P('tensor'), may hold values from 0.5 to 1.5
Outputs:
- mixed: bfloat16 [8192, 5120], P('patch', 'tensor')
The draws below stay inside these ranges and needn't reach their ends.
All inputs are finite; a program needn't handle non-finite values.
Results may differ from the reference program's by a relative error of at most 0.017.
Values may be sent and summed in bfloat16 or wider, within the bound.
A program may use at most 64 MiB of HBM per device.

```python
import jax
import jax.numpy as jnp
from jax import lax

D = 5120
HEAD_DIM = 128
HEADS = 24
TOK_DEV = 128
TOKENS = 8192


def shared_base(key):
    return jax.random.normal(key, (TOKENS, HEADS * HEAD_DIM), jnp.float32)


def draw_queries(key, part):
    base_draw = shared_base(key)
    key = jax.random.fold_in(key, 11)
    values = 2.5 * jnp.clip(jax.random.normal(key, base_draw.shape, jnp.float32), -6.0, 6.0)
    return values.astype(jnp.bfloat16)


def draw_stale_keys(key, part):
    base_draw = shared_base(key)
    values = jnp.clip(base_draw, -6.0, 6.0)
    return values.astype(jnp.bfloat16)


def raised(result, stream_key, source, target, parts, factor):
    owner, partner = [(jnp.arange(result.shape[position]) // (result.shape[position] // parts)).reshape([-1 if axis == position else 1 for axis in range(result.ndim)]) for position in (source, target)]
    chosen = jax.random.permutation(stream_key, parts)[partner]
    strong = (owner == chosen) | (owner == (partner + parts // 2) % parts)
    return jnp.where(strong, factor * result, result)


def block_scale(stream_key, dims, shards, smallest, top_value):
    level = 1.0
    for position, blocks in shards:
        steps = jax.random.uniform(jax.random.fold_in(jax.random.fold_in(stream_key, 6), position), (blocks,), jnp.float32, smallest / len(shards), top_value / len(shards))
        level = level * jnp.repeat(jnp.exp(steps), dims[position] // blocks).reshape((-1,) + (1,) * (len(dims) - 1 - position))
    return level


def scatter_about(own_key, dims, deviation, most, shards=(), held_as=jnp.bfloat16):
    result = jax.random.normal(own_key, dims, jnp.float32) * deviation
    if len(shards) > 0:
        result = block_scale(own_key, dims, shards, -0.22, 0.18) * result
    return jnp.clip(result, min=-most, max=most).astype(held_as)


def heavy_noise(rng, shape, spread, bound, cuts, heavy, kind=jnp.bfloat16):
    entries = spread * jax.random.normal(rng, shape, jnp.float32)
    if cuts:
        entries = entries * block_scale(rng, shape, cuts, -0.22, 0.18)
    return jnp.clip(raised(entries, jax.random.fold_in(rng, 3), *heavy), -bound, bound).astype(kind)


def setup_inputs(seed: int = 0) -> dict:
    key_of = jax.random.split(jax.random.key(seed), 9)
    return {
        "hidden_in": scatter_about(key_of[0], (TOKENS, D), 1.0, 6.0, ((0, 64), (1, 8))),
        "queries": draw_queries(jax.random.fold_in(key_of[8], 71), 0),
        "fresh_keys": scatter_about(key_of[2], (TOKENS, HEADS * HEAD_DIM), 1.0, 6.0, ((0, 64), (1, 8))),
        "fresh_values": scatter_about(key_of[3], (TOKENS, HEADS * HEAD_DIM), 1.0, 6.0, ((0, 64), (1, 8))),
        "stale_keys": draw_stale_keys(jax.random.fold_in(key_of[8], 71), 0),
        "stale_values": scatter_about(key_of[5], (TOKENS, HEADS * HEAD_DIM), 1.0, 6.0, ((0, 64), (1, 8))),
        "out_weight": heavy_noise(key_of[6], (HEADS * HEAD_DIM, D), (2 * HEAD_DIM) ** -0.5, 0.5, ((0, 8),), (0, 1, 8, 2.0)),
        "gate": jnp.clip(0.5 + 1.0 * jax.random.uniform(key_of[7], (D,), jnp.float32) ** block_scale(key_of[7], (D,), ((0, 8),), -0.2, 0.2), 0.5, 1.5),
    }


def reference(hidden_in, queries, fresh_keys, fresh_values, stale_keys, stale_values, out_weight, gate):
    block_count = TOKENS // TOK_DEV
    score_scale = HEAD_DIM ** -0.5

    def one_block(block_index):
        first_row = (block_index * TOK_DEV).astype(jnp.int32)
        query_block = lax.dynamic_slice_in_dim(queries, first_row, TOK_DEV, 0)
        query_heads = query_block.astype(jnp.float32).reshape(TOK_DEV, HEADS, HEAD_DIM)
        key_block = lax.dynamic_slice_in_dim(fresh_keys, first_row, TOK_DEV, 0)
        value_block = lax.dynamic_slice_in_dim(fresh_values, first_row, TOK_DEV, 0)
        all_keys = lax.dynamic_update_slice_in_dim(stale_keys, key_block, first_row, 0)
        all_values = lax.dynamic_update_slice_in_dim(stale_values, value_block, first_row, 0)
        key_heads = all_keys.astype(jnp.float32).reshape(TOKENS, HEADS, HEAD_DIM)
        value_heads = all_values.astype(jnp.float32).reshape(TOKENS, HEADS, HEAD_DIM)
        scores = jnp.einsum("thd,lhd->htl", query_heads, key_heads) * score_scale
        row_max = jnp.max(scores, axis=-1, keepdims=True)
        weights = jnp.exp(scores - row_max)
        denominator = jnp.sum(weights, axis=-1, keepdims=True)
        rounded = lax.optimization_barrier(weights.astype(jnp.bfloat16))
        summed = jnp.einsum("htl,lhd->htd", rounded.astype(jnp.float32), value_heads)
        attended_block = summed / denominator
        return attended_block.transpose(1, 0, 2).reshape(TOK_DEV, HEADS * HEAD_DIM).astype(jnp.bfloat16)

    attended = lax.map(one_block, jnp.arange(block_count, dtype=jnp.int32))
    attended = attended.reshape(TOKENS, HEADS * HEAD_DIM)
    projected = jnp.dot(attended, out_weight, preferred_element_type=jnp.float32)
    mixed = hidden_in.astype(jnp.float32) + gate[None, :] * projected
    return mixed.astype(jnp.bfloat16)
```

```python
import functools

import jax
import jax.numpy as jnp
from jax import lax
from jax.experimental import pallas as pl
from jax.experimental.pallas import tpu as pltpu
from jax.sharding import PartitionSpec as P

HEAD_DIM = 128
HEADS = 3
TOK = 128
COLS = 640
NY, NZ, NX = 4, 8, 4
SCALE = 1.4426950408889634 * HEAD_DIM**-0.5
MESH = pl.DeviceIdType.MESH
F32, BF16 = jnp.float32, jnp.bfloat16

ORDER = (
    (0, 1), (1, 1), (0, 2), (2, 1), (0, 3), (1, 2),
    (0, 4), (2, 2), (1, 3), (2, 3), (1, 4), (2, 4),
)


def flip(i, k):
    if k == 1:
        return i + 1 - 2 * (i % 2)
    if k == 2:
        return i + 2 - 4 * (i // 2)
    return 3 - i


def dot_t(a, b):
    return lax.dot_general(a, b, (((1,), (1,)), ((), ())), preferred_element_type=F32)


def dot(a, b):
    return jnp.dot(a, b, preferred_element_type=F32)


def kernel(
    hid, q, fk, fv, sk, sv, w, gate, out,
    kv, qb, m, l, acc, osend, orecv, att, attx, wb, pacc, ysend, yrecv, hidv, gatev,
    loc_sem, w_loc, z_send, z_recv, c_send, c_recv, q_send, q_recv, o_send, o_recv,
    a_send, a_recv, wx_send, wx_recv, wc_send, wc_recv, y_send, y_recv,
):
    p, t = lax.axis_index("patch"), lax.axis_index("tensor")
    y, z, c = p // (2 * NZ), (p // 2) % NZ, p % 2
    x, yh = t // 2, t % 2

    def dev(y, z, c, x, yh):
        return ((y * NZ + z) * 2 + c, x * 2 + yh)

    zp, zm = dev(y, (z + 1) % NZ, c, x, yh), dev(y, (z + NZ - 1) % NZ, c, x, yh)
    sib = dev(y, z, 1 - c, x, yh)
    ys = [None] + [dev(flip(y, k), z, c, x, yh) for k in (1, 2, 3)]
    xs = [None] + [dev(y, z, c, flip(x, k), yh) for k in (1, 2, 3)]
    mate = dev(y, z, c, x, 1 - yh)

    sent = []

    def rc(src, dst, ssem, rsem, to):
        return pltpu.make_async_remote_copy(
            src_ref=src, dst_ref=dst, send_sem=ssem, recv_sem=rsem,
            device_id=to, device_id_type=MESH,
        )

    def push(src, dst, ssem, rsem, to):
        copy = rc(src, dst, ssem, rsem, to)
        copy.start()
        sent.append(copy)

    def got(dst, ssem, rsem):
        rc(dst, dst, ssem, rsem, sib).wait_recv()

    def cols(h):
        return pl.ds(h * HEAD_DIM, HEAD_DIM)

    first, later = [], []
    for h in range(HEADS):
        for n, (src, dst) in enumerate((
            (sk.at[:, cols(h)], kv.at[h, 0, 0, 0]),
            (sv.at[:, cols(h)], kv.at[h, 0, 1, 0]),
            (q.at[:, cols(h)], qb.at[h, 0]),
        )):
            first.append(pltpu.make_async_copy(src, dst, loc_sem.at[h, n]))
    for h in range(HEADS):
        for n, (src, dst) in enumerate((
            (fk.at[:, cols(h)], kv.at[h, 0, 0, 2]),
            (fv.at[:, cols(h)], kv.at[h, 0, 1, 2]),
        )):
            later.append(pltpu.make_async_copy(src, dst, loc_sem.at[h, 3 + n]))
    own_cols = pl.ds(pl.multiple_of((2 * x + yh) * COLS, 128), COLS)
    mate_cols = pl.ds(pl.multiple_of((2 * x + 1 - yh) * COLS, 128), COLS)
    later.append(pltpu.make_async_copy(hid, hidv, loc_sem.at[0, 5]))
    later.append(pltpu.make_async_copy(gate, gatev, loc_sem.at[1, 5]))
    w_own = [
        pltpu.make_async_copy(w.at[:, :, own_cols], wb.at[0, :, 0], w_loc.at[0]),
        pltpu.make_async_copy(w.at[:, :, mate_cols], wb.at[1, :, 0], w_loc.at[1]),
    ]
    for copy in first:
        copy.start()

    barrier = pltpu.get_barrier_semaphore()
    peers = [zp, zm, sib, *ys[1:], *xs[1:], mate]
    for peer in peers:
        pl.semaphore_signal(barrier, inc=1, device_id=peer, device_id_type=MESH)
    for copy in first:
        copy.wait()
    pl.semaphore_wait(barrier, len(peers))

    def z_refs(h, d):
        if d < 4:
            return kv.at[h, d, :, 0], kv.at[h, d, :, 1]
        return kv.at[h, 4, 0, 0], kv.at[h, 4, 1, 0]

    def z_start(h, d):
        if d == 1:
            src = kv.at[h, 0, :, 0], kv.at[h, 0, :, 0]
        elif d < 4:
            src = kv.at[h, d - 1, :, 0], kv.at[h, d - 1, :, 1]
        else:
            src = kv.at[h, 3, 0, 0], kv.at[h, 3, 1, 1]
        dst = z_refs(h, d)
        for way, to in ((0, zp), (1, zm)):
            push(src[way], dst[way], z_send.at[way, h, d - 1], z_recv.at[way, h, d - 1], to)

    def c_refs(h, d):
        if d in (0, 4):
            return kv.at[h, d, :, 0], kv.at[h, d, :, 1]
        return kv.at[h, d, :, pl.ds(0, 2)], kv.at[h, d, :, pl.ds(2, 2)]

    def c_start(h, d):
        src, dst = c_refs(h, d)
        push(src, dst, c_send.at[h, d], c_recv.at[h, d], sib)

    def relay(h, d):
        dst = z_refs(h, d)
        for way in (0, 1):
            got(dst[way], z_send.at[way, h, d - 1], z_recv.at[way, h, d - 1])
        if d < 4:
            z_start(h, d + 1)
        c_start(h, d)

    def q_start(h):
        for k in (1, 2, 3):
            push(qb.at[h, 0], qb.at[h, k], q_send.at[h, k - 1], q_recv.at[h, k - 1], ys[k])

    def w_start(h):
        for k in (1, 2, 3):
            there = flip(x, k)
            half = (yh + c) % 2
            at = pl.ds(pl.multiple_of((2 * there + half) * COLS, 128), COLS)
            push(w.at[h, :, at], wb.at[c, h, k], wx_send.at[h, k - 1], wx_recv.at[h, k - 1], xs[k])

    def w_relay(h):
        for k in (1, 2, 3):
            got(wb.at[c, h, k], wx_send.at[h, k - 1], wx_recv.at[h, k - 1])
            push(wb.at[c, h, k], wb.at[c, h, k], wc_send.at[h, k - 1], wc_recv.at[h, k - 1], sib)

    def attend(h, rows, count, keys, values, fresh_start):
        qv = qb[h, pl.ds(rows, count)].reshape(count * TOK, HEAD_DIM)
        at = pl.ds(rows * TOK, count * TOK)
        s = dot_t(qv, keys) * SCALE
        top = jnp.max(s, axis=-1, keepdims=True)
        n = s.shape[1] // 128
        if fresh_start:
            m_new = jnp.broadcast_to(top, (count * TOK, 128))
        else:
            m_old = m[h, at, :]
            m_new = jnp.maximum(m_old, top)
            alpha = jnp.exp2(m_old - m_new)
        parts = [jnp.exp2(s[:, j * 128 : (j + 1) * 128] - m_new) for j in range(n)]
        total = functools.reduce(jnp.add, parts)
        pv = dot(jnp.concatenate([e.astype(BF16) for e in parts], axis=1), values)
        m[h, at, :] = m_new
        if fresh_start:
            l[h, at, :] = total
            acc[h, at, :] = pv
        else:
            l[h, at, :] = alpha * l[h, at, :] + total
            acc[h, at, :] = alpha * acc[h, at, :] + pv

    def work(h, d):
        src, dst = c_refs(h, d)
        got(dst, c_send.at[h, d], c_recv.at[h, d])
        if d == 0:
            for k in (1, 2, 3):
                got(qb.at[h, k], q_send.at[h, k - 1], q_recv.at[h, k - 1])
            both = kv[h, 0, :, pl.ds(1, 2)]
            attend(h, 0, 1, both[0].reshape(-1, 128), both[1].reshape(-1, 128), True)
            both = kv[h, 0, :, pl.ds(0, 2)]
            attend(h, 1, 3, both[0].reshape(-1, 128), both[1].reshape(-1, 128), True)
        else:
            n = 2 if d == 4 else 4
            keys = kv[h, d, 0, pl.ds(0, n)].reshape(n * TOK, 128)
            values = kv[h, d, 1, pl.ds(0, n)].reshape(n * TOK, 128)
            for r in (0, 2):
                attend(h, r, 2, keys, values, False)

    def finish(h):
        for k in (1, 2, 3, 0):
            at = pl.ds(k * TOK, TOK)
            total = jnp.sum(l[h, at, :], axis=-1, keepdims=True)
            o = acc[h, at, :] * (1.0 / total)
            lse = m[h, at, :] + jnp.log2(total)
            if k == 0:
                acc[h, at, :] = o
                m[h, at, :] = lse
                continue
            osend[h, k - 1, pl.ds(0, TOK), :] = o.astype(BF16)
            flat = lse.T[:16, :]
            hi = flat.astype(BF16)
            rest = flat - hi.astype(F32)
            mid = rest.astype(BF16)
            low = (rest - mid.astype(F32)).astype(BF16)
            row = lax.broadcasted_iota(jnp.int32, (16, 128), 0)
            three = jnp.where(
                row == 0, hi.astype(F32), jnp.where(row == 1, mid.astype(F32), low.astype(F32))
            )
            osend[h, k - 1, pl.ds(TOK, 16), :] = three.astype(BF16)
            push(
                osend.at[h, k - 1], orecv.at[h, k - 1],
                o_send.at[h, k - 1], o_recv.at[h, k - 1], ys[k],
            )

    def merge(h):
        own = pl.ds(0, TOK)
        os, lses = [acc[h, own, :]], [m[h, own, :]]
        for k in (1, 2, 3):
            got(orecv.at[h, k - 1], o_send.at[h, k - 1], o_recv.at[h, k - 1])
            os.append(orecv[h, k - 1, pl.ds(0, TOK), :].astype(F32))
            three = orecv[h, k - 1, pl.ds(TOK, 16), :].astype(F32)
            flat = three[0:1] + three[1:2] + three[2:3]
            lses.append(jnp.broadcast_to(flat, (TOK, 128)).T)
        top = functools.reduce(jnp.maximum, lses)
        ws = [jnp.exp2(e - top) for e in lses]
        den = functools.reduce(jnp.add, ws)
        num = functools.reduce(jnp.add, [a * b for a, b in zip(ws, os, strict=True)])
        result = (num / den).astype(BF16)
        att[h] = result
        attx[h, :, pl.ds(0, 128)] = result
        for k in (1, 2, 3):
            push(
                att.at[h], attx.at[h, :, pl.ds(k * 128, 128)],
                a_send.at[h, k - 1], a_recv.at[h, k - 1], xs[k],
            )

    def project(h):
        for k in (1, 2, 3):
            got(attx.at[h, :, pl.ds(k * 128, 128)], a_send.at[h, k - 1], a_recv.at[h, k - 1])
            got(wb.at[1 - c, h, k], wc_send.at[h, k - 1], wc_recv.at[h, k - 1])
        a = attx[h]
        for part in (1, 0):
            term = dot(a, wb[part, h].reshape(NX * TOK, COLS))
            if h > 0:
                term = pacc[part] + term
            if h < HEADS - 1 or part == 0:
                pacc[part] = term
            else:
                ysend[...] = term.astype(BF16)
                push(ysend, yrecv, y_send, y_recv, mate)

    z_start(0, 1)
    q_start(0)
    z_start(1, 1)
    for h in range(HEADS):
        c_start(h, 0)
    q_start(1)
    z_start(2, 1)
    q_start(2)
    for copy in later:
        copy.start()
    for h in range(HEADS):
        w_start(h)
    for copy in w_own:
        copy.start()
    for copy in later:
        copy.wait()

    todo = {i: [] for i in range(len(ORDER) + 1)}
    todo[1].append((0, 0))
    todo[2].append((0, 1))
    todo[3].append((1, 0))
    todo[4].append((1, 1))
    todo[5].append((0, 2))
    todo[6].append((2, 0))
    todo[7].append((0, 3))
    todo[7].append((2, 1))
    todo[8].append((0, 4))
    todo[8].append((1, 2))
    todo[9].append((2, 2))
    todo[10].append((1, 3))
    todo[11].append((2, 3))
    todo[11].append((1, 4))
    todo[12].append((2, 4))
    for i in range(len(ORDER) + 1):
        if i < len(ORDER):
            relay(*ORDER[i])
        for h, d in todo[i]:
            work(h, d)
            if d == 4:
                finish(h)
        if i == 9:
            w_relay(0)
        if i == 11:
            merge(0)
    w_relay(1)
    merge(1)
    for copy in w_own:
        copy.wait()
    project(0)
    merge(2)
    w_relay(2)
    project(1)
    project(2)
    got(yrecv, y_send, y_recv)
    projected = pacc[0] + yrecv[...].astype(F32)
    mixed = hidv[...].astype(F32) + gatev[...] * projected
    out[...] = mixed.astype(BF16)
    for copy in sent:
        copy.wait_send()


def local(hidden_in, queries, fresh_keys, fresh_values, stale_keys, stale_values, out_weight, gate):
    anywhere = pl.BlockSpec(memory_space=pl.ANY)
    vmem, dma = pltpu.VMEM, pltpu.SemaphoreType.DMA
    wide = (HEADS, NY * TOK, 128)
    return pl.pallas_call(
        kernel,
        out_shape=jax.ShapeDtypeStruct((TOK, COLS), BF16),
        in_specs=[anywhere] * 8,
        out_specs=pl.BlockSpec(memory_space=pltpu.VMEM),
        scratch_shapes=[
            vmem((HEADS, 5, 2, 4, TOK, 128), BF16),
            vmem((HEADS, NY, TOK, 128), BF16),
            vmem(wide, F32),
            vmem(wide, F32),
            vmem(wide, F32),
            vmem((HEADS, 3, TOK + 16, 128), BF16),
            vmem((HEADS, 3, TOK + 16, 128), BF16),
            vmem((HEADS, TOK, 128), BF16),
            vmem((HEADS, TOK, NX * 128), BF16),
            vmem((2, HEADS, NX, TOK, COLS), BF16),
            vmem((2, TOK, COLS), F32),
            vmem((TOK, COLS), BF16),
            vmem((TOK, COLS), BF16),
            vmem((TOK, COLS), BF16),
            vmem((1, COLS), F32),
            dma((HEADS, 6)),
            dma((2,)),
            dma((2, HEADS, 4)),
            dma((2, HEADS, 4)),
            dma((HEADS, 5)),
            dma((HEADS, 5)),
            *[dma((HEADS, 3)) for _ in range(10)],
            dma(()),
            dma(()),
        ],
        compiler_params=pltpu.CompilerParams(
            collective_id=0, has_side_effects=True, vmem_limit_bytes=40 * 2**20
        ),
    )(
        hidden_in, queries, fresh_keys, fresh_values, stale_keys, stale_values,
        out_weight.reshape(HEADS, TOK, -1), gate.reshape(1, COLS),
    )


def solution(mesh):
    split = P("patch", "tensor")
    return jax.shard_map(
        local,
        mesh=mesh,
        in_specs=(split,) * 6 + (P("tensor", None), P("tensor")),
        out_specs=split,
        check_vma=False,
    )
```

```python
import functools

import jax
import jax.numpy as jnp
from jax import lax
from jax.experimental import pallas as pl
from jax.experimental.pallas import tpu as pltpu
from jax.sharding import PartitionSpec as P

HEAD_DIM = 128
HEADS = 3
TOK = 128
COLS = 640
NY, NZ, NX = 4, 8, 4
SCALE = 1.4426950408889634 * HEAD_DIM**-0.5
MESH = pl.DeviceIdType.MESH
F32, BF16 = jnp.float32, jnp.bfloat16

ORDER = (
    (0, 1), (1, 1), (0, 2), (2, 1), (0, 3), (1, 2),
    (0, 4), (2, 2), (1, 3), (2, 3), (1, 4), (2, 4),
)


def flip(i, k):
    if k == 1:
        return i + 1 - 2 * (i % 2)
    if k == 2:
        return i + 2 - 4 * (i // 2)
    return 3 - i


def dot_t(a, b):
    return lax.dot_general(a, b, (((1,), (1,)), ((), ())), preferred_element_type=F32)


def dot(a, b):
    return jnp.dot(a, b, preferred_element_type=F32)


def kernel(
    hid, q, fk, fv, sk, sv, w, gate, out,
    kv, qb, m, l, acc, osend, orecv, att, attx, wb, pacc, ysend, yrecv, hidv, gatev,
    loc_sem, w_loc, z_send, z_recv, c_send, c_recv, q_send, q_recv, o_send, o_recv,
    a_send, a_recv, wx_send, wx_recv, wc_send, wc_recv, y_send, y_recv,
):
    p, t = lax.axis_index("patch"), lax.axis_index("tensor")
    y, z, c = p // (2 * NZ), (p // 2) % NZ, p % 2
    x, yh = t // 2, t % 2

    def dev(y, z, c, x, yh):
        return ((y * NZ + z) * 2 + c, x * 2 + yh)

    zp, zm = dev(y, (z + 1) % NZ, c, x, yh), dev(y, (z + NZ - 1) % NZ, c, x, yh)
    sib = dev(y, z, 1 - c, x, yh)
    ys = [None] + [dev(flip(y, k), z, c, x, yh) for k in (1, 2, 3)]
    xs = [None] + [dev(y, z, c, flip(x, k), yh) for k in (1, 2, 3)]
    mate = dev(y, z, c, x, 1 - yh)

    sent = []

    def rc(src, dst, ssem, rsem, to):
        return pltpu.make_async_remote_copy(
            src_ref=src, dst_ref=dst, send_sem=ssem, recv_sem=rsem,
            device_id=to, device_id_type=MESH,
        )

    def push(src, dst, ssem, rsem, to):
        copy = rc(src, dst, ssem, rsem, to)
        copy.start()
        sent.append(copy)

    def got(dst, ssem, rsem):
        rc(dst, dst, ssem, rsem, sib).wait_recv()

    def cols(h):
        return pl.ds(h * HEAD_DIM, HEAD_DIM)

    first, later = [], []
    for h in range(HEADS):
        for n, (src, dst) in enumerate((
            (sk.at[:, cols(h)], kv.at[h, 0, 0, 0]),
            (sv.at[:, cols(h)], kv.at[h, 0, 1, 0]),
            (q.at[:, cols(h)], qb.at[h, 0]),
        )):
            first.append(pltpu.make_async_copy(src, dst, loc_sem.at[h, n]))
    for h in range(HEADS):
        for n, (src, dst) in enumerate((
            (fk.at[:, cols(h)], kv.at[h, 0, 0, 2]),
            (fv.at[:, cols(h)], kv.at[h, 0, 1, 2]),
        )):
            later.append(pltpu.make_async_copy(src, dst, loc_sem.at[h, 3 + n]))
    own_cols = pl.ds(pl.multiple_of((2 * x + yh) * COLS, 128), COLS)
    mate_cols = pl.ds(pl.multiple_of((2 * x + 1 - yh) * COLS, 128), COLS)
    later.append(pltpu.make_async_copy(hid, hidv, loc_sem.at[0, 5]))
    later.append(pltpu.make_async_copy(gate, gatev, loc_sem.at[1, 5]))
    w_own = [
        pltpu.make_async_copy(w.at[:, :, own_cols], wb.at[0, :, 0], w_loc.at[0]),
        pltpu.make_async_copy(w.at[:, :, mate_cols], wb.at[1, :, 0], w_loc.at[1]),
    ]
    for copy in first:
        copy.start()

    barrier = pltpu.get_barrier_semaphore()
    peers = [zp, zm, sib, *ys[1:], *xs[1:], mate]
    for peer in peers:
        pl.semaphore_signal(barrier, inc=1, device_id=peer, device_id_type=MESH)
    for copy in first:
        copy.wait()
    pl.semaphore_wait(barrier, len(peers))

    def z_refs(h, d):
        if d < 4:
            return kv.at[h, d, :, 0], kv.at[h, d, :, 1]
        return kv.at[h, 4, 0, 0], kv.at[h, 4, 1, 0]

    def z_start(h, d):
        if d == 1:
            src = kv.at[h, 0, :, 0], kv.at[h, 0, :, 0]
        elif d < 4:
            src = kv.at[h, d - 1, :, 0], kv.at[h, d - 1, :, 1]
        else:
            src = kv.at[h, 3, 0, 0], kv.at[h, 3, 1, 1]
        dst = z_refs(h, d)
        for way, to in ((0, zp), (1, zm)):
            push(src[way], dst[way], z_send.at[way, h, d - 1], z_recv.at[way, h, d - 1], to)

    def c_refs(h, d):
        if d in (0, 4):
            return kv.at[h, d, :, 0], kv.at[h, d, :, 1]
        return kv.at[h, d, :, pl.ds(0, 2)], kv.at[h, d, :, pl.ds(2, 2)]

    def c_start(h, d):
        src, dst = c_refs(h, d)
        push(src, dst, c_send.at[h, d], c_recv.at[h, d], sib)

    def relay(h, d):
        dst = z_refs(h, d)
        for way in (0, 1):
            got(dst[way], z_send.at[way, h, d - 1], z_recv.at[way, h, d - 1])
        if d < 4:
            z_start(h, d + 1)
        c_start(h, d)

    def q_start(h):
        for k in (1, 2, 3):
            push(qb.at[h, 0], qb.at[h, k], q_send.at[h, k - 1], q_recv.at[h, k - 1], ys[k])

    def w_start(h):
        for k in (1, 2, 3):
            there = flip(x, k)
            half = (yh + c) % 2
            at = pl.ds(pl.multiple_of((2 * there + half) * COLS, 128), COLS)
            push(w.at[h, :, at], wb.at[c, h, k], wx_send.at[h, k - 1], wx_recv.at[h, k - 1], xs[k])

    def w_relay(h):
        for k in (1, 2, 3):
            got(wb.at[c, h, k], wx_send.at[h, k - 1], wx_recv.at[h, k - 1])
            push(wb.at[c, h, k], wb.at[c, h, k], wc_send.at[h, k - 1], wc_recv.at[h, k - 1], sib)

    def attend(h, rows, count, keys, values, fresh_start):
        qv = qb[h, pl.ds(rows, count)].reshape(count * TOK, HEAD_DIM)
        at = pl.ds(rows * TOK, count * TOK)
        s = dot_t(qv, keys) * SCALE
        top = jnp.max(s, axis=-1, keepdims=True)
        n = s.shape[1] // 128
        if fresh_start:
            m_new = jnp.broadcast_to(top, (count * TOK, 128))
        else:
            m_old = m[h, at, :]
            m_new = jnp.maximum(m_old, top)
            alpha = jnp.exp2(m_old - m_new)
        parts = [jnp.exp2(s[:, j * 128 : (j + 1) * 128] - m_new) for j in range(n)]
        total = functools.reduce(jnp.add, parts)
        pv = dot(jnp.concatenate([e.astype(BF16) for e in parts], axis=1), values)
        m[h, at, :] = m_new
        if fresh_start:
            l[h, at, :] = total
            acc[h, at, :] = pv
        else:
            l[h, at, :] = alpha * l[h, at, :] + total
            acc[h, at, :] = alpha * acc[h, at, :] + pv

    def work(h, d):
        src, dst = c_refs(h, d)
        got(dst, c_send.at[h, d], c_recv.at[h, d])
        if d == 0:
            for k in (1, 2, 3):
                got(qb.at[h, k], q_send.at[h, k - 1], q_recv.at[h, k - 1])
            both = kv[h, 0, :, pl.ds(1, 2)]
            attend(h, 0, 1, both[0].reshape(-1, 128), both[1].reshape(-1, 128), True)
            both = kv[h, 0, :, pl.ds(0, 2)]
            attend(h, 1, 3, both[0].reshape(-1, 128), both[1].reshape(-1, 128), True)
        else:
            n = 2 if d == 4 else 4
            keys = kv[h, d, 0, pl.ds(0, n)].reshape(n * TOK, 128)
            values = kv[h, d, 1, pl.ds(0, n)].reshape(n * TOK, 128)
            for r in (0, 2):
                attend(h, r, 2, keys, values, False)

    def finish(h):
        for k in (1, 2, 3, 0):
            at = pl.ds(k * TOK, TOK)
            total = jnp.sum(l[h, at, :], axis=-1, keepdims=True)
            o = acc[h, at, :] * (1.0 / total)
            lse = m[h, at, :] + jnp.log2(total)
            if k == 0:
                acc[h, at, :] = o
                m[h, at, :] = lse
                continue
            osend[h, k - 1, pl.ds(0, TOK), :] = o.astype(BF16)
            flat = lse.T[:16, :]
            hi = flat.astype(BF16)
            rest = flat - hi.astype(F32)
            mid = rest.astype(BF16)
            low = (rest - mid.astype(F32)).astype(BF16)
            row = lax.broadcasted_iota(jnp.int32, (16, 128), 0)
            three = jnp.where(
                row == 0, hi.astype(F32), jnp.where(row == 1, mid.astype(F32), low.astype(F32))
            )
            osend[h, k - 1, pl.ds(TOK, 16), :] = three.astype(BF16)
            push(
                osend.at[h, k - 1], orecv.at[h, k - 1],
                o_send.at[h, k - 1], o_recv.at[h, k - 1], ys[k],
            )

    def merge(h):
        own = pl.ds(0, TOK)
        os, lses = [acc[h, own, :]], [m[h, own, :]]
        for k in (1, 2, 3):
            got(orecv.at[h, k - 1], o_send.at[h, k - 1], o_recv.at[h, k - 1])
            os.append(orecv[h, k - 1, pl.ds(0, TOK), :].astype(F32))
            three = orecv[h, k - 1, pl.ds(TOK, 16), :].astype(F32)
            flat = three[0:1] + three[1:2] + three[2:3]
            lses.append(jnp.broadcast_to(flat, (TOK, 128)).T)
        top = functools.reduce(jnp.maximum, lses)
        ws = [jnp.exp2(e - top) for e in lses]
        den = functools.reduce(jnp.add, ws)
        num = functools.reduce(jnp.add, [a * b for a, b in zip(ws, os, strict=True)])
        result = (num / den).astype(BF16)
        att[h] = result
        attx[h, :, pl.ds(0, 128)] = result
        for k in (1, 2, 3):
            push(
                att.at[h], attx.at[h, :, pl.ds(k * 128, 128)],
                a_send.at[h, k - 1], a_recv.at[h, k - 1], xs[k],
            )

    def project(h):
        for k in (1, 2, 3):
            got(attx.at[h, :, pl.ds(k * 128, 128)], a_send.at[h, k - 1], a_recv.at[h, k - 1])
            got(wb.at[1 - c, h, k], wc_send.at[h, k - 1], wc_recv.at[h, k - 1])
        a = attx[h]
        for part in (1, 0):
            term = dot(a, wb[part, h].reshape(NX * TOK, COLS))
            if h > 0:
                term = pacc[part] + term
            if h < HEADS - 1 or part == 0:
                pacc[part] = term
            else:
                ysend[...] = term.astype(BF16)
                push(ysend, yrecv, y_send, y_recv, mate)

    z_start(0, 1)
    q_start(0)
    z_start(1, 1)
    for h in range(HEADS):
        c_start(h, 0)
    q_start(1)
    z_start(2, 1)
    q_start(2)
    for copy in later:
        copy.start()
    for h in range(HEADS):
        w_start(h)
    for copy in w_own:
        copy.start()
    for copy in later:
        copy.wait()

    todo = {i: [] for i in range(len(ORDER) + 1)}
    todo[1].append((0, 0))
    todo[2].append((0, 1))
    todo[3].append((1, 0))
    todo[4].append((1, 1))
    todo[5].append((0, 2))
    todo[6].append((2, 0))
    todo[7].append((0, 3))
    todo[7].append((2, 1))
    todo[8].append((0, 4))
    todo[8].append((1, 2))
    todo[9].append((2, 2))
    todo[10].append((1, 3))
    todo[11].append((2, 3))
    todo[11].append((1, 4))
    todo[12].append((2, 4))
    for i in range(len(ORDER) + 1):
        if i < len(ORDER):
            relay(*ORDER[i])
        for h, d in todo[i]:
            work(h, d)
            if d == 4:
                finish(h)
        if i == 9:
            w_relay(0)
        if i == 11:
            merge(0)
    w_relay(1)
    merge(1)
    for copy in w_own:
        copy.wait()
    project(0)
    merge(2)
    w_relay(2)
    project(1)
    project(2)
    got(yrecv, y_send, y_recv)
    projected = pacc[0] + yrecv[...].astype(F32)
    mixed = hidv[...].astype(F32) + gatev[...][None, :] * projected
    out[...] = mixed.astype(BF16)
    for copy in sent:
        copy.wait_send()


def local(hidden_in, queries, fresh_keys, fresh_values, stale_keys, stale_values, out_weight, gate):
    anywhere = pl.BlockSpec(memory_space=pltpu.HBM)
    vmem, dma = pltpu.VMEM, pltpu.SemaphoreType.DMA
    wide = (HEADS, NY * TOK, 128)
    return pl.pallas_call(
        kernel,
        out_shape=jax.ShapeDtypeStruct((TOK, COLS), BF16),
        in_specs=[anywhere] * 8,
        out_specs=pl.BlockSpec(memory_space=pltpu.VMEM),
        scratch_shapes=[
            vmem((HEADS, 5, 2, 4, TOK, 128), BF16),
            vmem((HEADS, NY, TOK, 128), BF16),
            vmem(wide, F32),
            vmem(wide, F32),
            vmem(wide, F32),
            vmem((HEADS, 3, TOK + 16, 128), BF16),
            vmem((HEADS, 3, TOK + 16, 128), BF16),
            vmem((HEADS, TOK, 128), BF16),
            vmem((HEADS, TOK, NX * 128), BF16),
            vmem((2, HEADS, NX, TOK, COLS), BF16),
            vmem((2, TOK, COLS), F32),
            vmem((TOK, COLS), BF16),
            vmem((TOK, COLS), BF16),
            vmem((TOK, COLS), BF16),
            vmem((COLS,), F32),
            dma((HEADS, 6)),
            dma((2,)),
            dma((2, HEADS, 4)),
            dma((2, HEADS, 4)),
            dma((HEADS, 5)),
            dma((HEADS, 5)),
            *[dma((HEADS, 3)) for _ in range(10)],
            dma(()),
            dma(()),
        ],
        compiler_params=pltpu.CompilerParams(
            collective_id=0, has_side_effects=True, vmem_limit_bytes=62 * 2**20
        ),
    )(
        hidden_in, queries, fresh_keys, fresh_values, stale_keys, stale_values,
        out_weight.reshape(HEADS, TOK, -1), gate,
    )


def solution(mesh):
    split = P("patch", "tensor")
    return jax.shard_map(
        local,
        mesh=mesh,
        in_specs=(split,) * 6 + (P("tensor", None), P("tensor")),
        out_specs=split,
        check_vma=False,
    )
```

```python
import functools

import jax
import jax.numpy as jnp
from jax import lax
from jax.experimental import pallas as pl
from jax.experimental.pallas import tpu as pltpu
from jax.sharding import PartitionSpec as P

HEAD_DIM = 128
HEADS = 3
TOK = 128
COLS = 640
NY, NZ, NX = 4, 8, 4
SCALE = 1.4426950408889634 * HEAD_DIM**-0.5
MESH = pl.DeviceIdType.MESH
HALF = TOK // 2
PART = HALF + 16
F32, BF16 = jnp.float32, jnp.bfloat16

ORDER = ((0, 1), (1, 1), (0, 2), (2, 1), (0, 3), (1, 2), (0, 4), (2, 2), (1, 3), (2, 3), (1, 4), (2, 4))


def flip(i, k):
    if k == 1:
        return i + 1 - 2 * (i % 2)
    if k == 2:
        return i + 2 - 4 * (i // 2)
    return 3 - i


def dot_t(a, b):
    return lax.dot_general(a, b, (((1,), (1,)), ((), ())), preferred_element_type=F32)


def dot(a, b):
    return jnp.dot(a, b, preferred_element_type=F32)


def kernel(
    hid, q, fk, fv, sk, sv, w, gate, out,
    kv, qb, m, l, acc, osend, orecv, att, attx, wb, pacc, ysend, yrecv, hidv, gatev,
    loc_sem, w_loc, z_send, z_recv, c_send, c_recv, q_send, q_recv, o_send, o_recv,
    a_send, a_recv, wx_send, wx_recv, wc_send, wc_recv, y_send, y_recv,
):
    p, t = lax.axis_index("patch"), lax.axis_index("tensor")
    y, z, c = p // (2 * NZ), (p // 2) % NZ, p % 2
    x, yh = t // 2, t % 2

    def dev(y, z, c, x, yh):
        return ((y * NZ + z) * 2 + c, x * 2 + yh)

    zp, zm = dev(y, (z + 1) % NZ, c, x, yh), dev(y, (z + NZ - 1) % NZ, c, x, yh)
    sib = dev(y, z, 1 - c, x, yh)
    ys = [None] + [dev(flip(y, k), z, c, x, yh) for k in (1, 2, 3)]
    xs = [None] + [dev(y, z, c, flip(x, k), yh) for k in (1, 2, 3)]
    mate = dev(y, z, c, x, 1 - yh)

    sent = []

    def rc(src, dst, ssem, rsem, to):
        return pltpu.make_async_remote_copy(
            src_ref=src, dst_ref=dst, send_sem=ssem, recv_sem=rsem,
            device_id=to, device_id_type=MESH,
        )

    def push(src, dst, ssem, rsem, to):
        copy = rc(src, dst, ssem, rsem, to)
        copy.start()
        sent.append(copy)

    def got(dst, ssem, rsem):
        rc(dst, dst, ssem, rsem, sib).wait_recv()

    barrier = pltpu.get_barrier_semaphore()
    peers = [zp, zm, sib, *ys[1:], *xs[1:], mate]
    for peer in peers:
        pl.semaphore_signal(barrier, inc=1, device_id=peer, device_id_type=MESH)

    def cols(h):
        return pl.ds(h * HEAD_DIM, HEAD_DIM)

    first, later = [], []
    for h in range(HEADS):
        for n, (src, dst) in enumerate((
            (sk.at[:, cols(h)], kv.at[h, 0, 0, 0]),
            (sv.at[:, cols(h)], kv.at[h, 0, 1, 0]),
            (q.at[:, cols(h)], qb.at[h, 0]),
        )):
            first.append(pltpu.make_async_copy(src, dst, loc_sem.at[h, n]))
    for h in range(HEADS):
        for n, (src, dst) in enumerate((
            (fk.at[:, cols(h)], kv.at[h, 0, 0, 2]),
            (fv.at[:, cols(h)], kv.at[h, 0, 1, 2]),
        )):
            later.append(pltpu.make_async_copy(src, dst, loc_sem.at[h, 3 + n]))
    own_cols = pl.ds(pl.multiple_of((2 * x + yh) * COLS, 128), COLS)
    mate_cols = pl.ds(pl.multiple_of((2 * x + 1 - yh) * COLS, 128), COLS)
    later.append(pltpu.make_async_copy(hid, hidv, loc_sem.at[0, 5]))
    later.append(pltpu.make_async_copy(gate, gatev, loc_sem.at[1, 5]))
    w_own = [
        pltpu.make_async_copy(w.at[:, :, own_cols], wb.at[0, :, 0], w_loc.at[0]),
        pltpu.make_async_copy(w.at[:, :, mate_cols], wb.at[1, :, 0], w_loc.at[1]),
    ]
    for copy in first + later + w_own:
        copy.start()

    for copy in first:
        copy.wait()
    pl.semaphore_wait(barrier, len(peers))

    def z_refs(h, d):
        if d < 4:
            return kv.at[h, d, :, 0], kv.at[h, d, :, 1]
        return kv.at[h, 4, 0, 0], kv.at[h, 4, 1, 0]

    def z_start(h, d, way):
        if d == 1:
            src = kv.at[h, 0, :, 0], kv.at[h, 0, :, 0]
        elif d < 4:
            src = kv.at[h, d - 1, :, 0], kv.at[h, d - 1, :, 1]
        else:
            src = kv.at[h, 3, 0, 0], kv.at[h, 3, 1, 1]
        dst = z_refs(h, d)
        to = (zp, zm)[way]
        push(src[way], dst[way], z_send.at[way, h, d - 1], z_recv.at[way, h, d - 1], to)

    def c_refs(h, d):
        if d in (0, 4):
            return kv.at[h, d, :, 0], kv.at[h, d, :, 1]
        return kv.at[h, d, :, pl.ds(0, 2)], kv.at[h, d, :, pl.ds(2, 2)]

    def c_start(h, d):
        src, dst = c_refs(h, d)
        push(src, dst, c_send.at[h, d], c_recv.at[h, d], sib)

    def relay(h, d):
        dst = z_refs(h, d)
        for way in (0, 1):
            got(dst[way], z_send.at[way, h, d - 1], z_recv.at[way, h, d - 1])
            if d < 4:
                z_start(h, d + 1, way)
        c_start(h, d)

    def q_start(h):
        for k in (1, 2, 3):
            push(qb.at[h, 0], qb.at[h, k], q_send.at[h, k - 1], q_recv.at[h, k - 1], ys[k])

    def w_start(h):
        for k in (1, 2, 3):
            there = flip(x, k)
            half = (yh + c) % 2
            at = pl.ds(pl.multiple_of((2 * there + half) * COLS, 128), COLS)
            push(w.at[h, :, at], wb.at[c, h, k], wx_send.at[h, k - 1], wx_recv.at[h, k - 1], xs[k])

    def w_relay(h):
        for k in (1, 2, 3):
            got(wb.at[c, h, k], wx_send.at[h, k - 1], wx_recv.at[h, k - 1])
            push(wb.at[c, h, k], wb.at[c, h, k], wc_send.at[h, k - 1], wc_recv.at[h, k - 1], sib)

    def attend(h, rows, count, keys, values, fresh_start):
        qv = qb[h, pl.ds(rows, count)].reshape(count * TOK, HEAD_DIM)
        at = pl.ds(rows * TOK, count * TOK)
        s = dot_t(qv, keys) * SCALE
        top = jnp.max(s, axis=-1, keepdims=True)
        n = s.shape[1] // 128
        if fresh_start:
            m_new = jnp.broadcast_to(top, (count * TOK, 128))
        else:
            m_old = m[h, at, :]
            m_new = jnp.maximum(m_old, top)
            alpha = jnp.exp2(m_old - m_new)
        parts = [jnp.exp2(s[:, j * 128 : (j + 1) * 128] - m_new) for j in range(n)]
        total = functools.reduce(jnp.add, parts)
        pv = dot(jnp.concatenate([e.astype(BF16) for e in parts], axis=1), values)
        m[h, at, :] = m_new
        if fresh_start:
            l[h, at, :] = total
            acc[h, at, :] = pv
        else:
            l[h, at, :] = alpha * l[h, at, :] + total
            acc[h, at, :] = alpha * acc[h, at, :] + pv

    def work(h, d):
        src, dst = c_refs(h, d)
        got(dst, c_send.at[h, d], c_recv.at[h, d])
        if d == 0:
            for k in (1, 2, 3):
                got(qb.at[h, k], q_send.at[h, k - 1], q_recv.at[h, k - 1])
            both = kv[h, 0, :, pl.ds(1, 2)]
            attend(h, 0, 1, both[0].reshape(-1, 128), both[1].reshape(-1, 128), True)
            both = kv[h, 0, :, pl.ds(0, 2)]
            attend(h, 1, 3, both[0].reshape(-1, 128), both[1].reshape(-1, 128), True)
        else:
            n = 2 if d == 4 else 4
            keys = kv[h, d, 0, pl.ds(0, n)].reshape(n * TOK, 128)
            values = kv[h, d, 1, pl.ds(0, n)].reshape(n * TOK, 128)
            for r in (0, 2):
                attend(h, r, 2, keys, values, False)

    def o_copy(h, k, r):
        at = pl.ds(r * PART, PART)
        return (
            osend.at[h, k - 1, at], orecv.at[h, k - 1, at],
            o_send.at[r, h, k - 1], o_recv.at[r, h, k - 1],
        )

    def finish(h):
        for k in (1, 2, 3, 0):
            at = pl.ds(k * TOK, TOK)
            total = jnp.sum(l[h, at, :], axis=-1, keepdims=True)
            o = acc[h, at, :] * (1.0 / total)
            lse = m[h, at, :] + jnp.log2(total)
            if k == 0:
                acc[h, at, :] = o
                m[h, at, :] = lse
                continue
            o = o.astype(BF16)
            flat = lse.T[:16, :]
            hi = flat.astype(BF16)
            rest = flat - hi.astype(F32)
            mid = rest.astype(BF16)
            low = (rest - mid.astype(F32)).astype(BF16)
            row = lax.broadcasted_iota(jnp.int32, (16, 128), 0)
            three = jnp.where(
                row == 0, hi.astype(F32), jnp.where(row == 1, mid.astype(F32), low.astype(F32))
            ).astype(BF16)
            for r in (0, 1):
                osend[h, k - 1, pl.ds(r * PART, HALF), :] = o[r * HALF : (r + 1) * HALF]
                osend[h, k - 1, pl.ds(r * PART + HALF, 16), :] = three
            push(*o_copy(h, k, 0), ys[k])
        for k in (1, 2, 3):
            push(*o_copy(h, k, 1), ys[k])

    def a_copy(h, k, r):
        rows = pl.ds(r * HALF, HALF)
        return (
            att.at[h, rows], attx.at[h, rows, pl.ds(k * 128, 128)],
            a_send.at[r, h, k - 1], a_recv.at[r, h, k - 1],
        )

    def merge(h, r):
        own = pl.ds(r * HALF, HALF)
        os, lses = [acc[h, own, :]], [m[h, own, :]]
        for k in (1, 2, 3):
            _, dst, ssem, rsem = o_copy(h, k, r)
            got(dst, ssem, rsem)
            os.append(orecv[h, k - 1, pl.ds(r * PART, HALF), :].astype(F32))
            three = orecv[h, k - 1, pl.ds(r * PART + HALF, 16), :].astype(F32)
            flat = three[0:1] + three[1:2] + three[2:3]
            lses.append(jnp.broadcast_to(flat, (TOK, 128)).T[r * HALF : (r + 1) * HALF])
        top = functools.reduce(jnp.maximum, lses)
        ws = [jnp.exp2(e - top) for e in lses]
        den = functools.reduce(jnp.add, ws)
        num = functools.reduce(jnp.add, [a * b for a, b in zip(ws, os, strict=True)])
        result = (num / den).astype(BF16)
        att[h, own, :] = result
        attx[h, own, pl.ds(0, 128)] = result
        for k in (1, 2, 3):
            push(*a_copy(h, k, r), xs[k])

    def await_att(h, r):
        for k in (1, 2, 3):
            _, dst, ssem, rsem = a_copy(h, k, r)
            got(dst, ssem, rsem)

    def await_w(h):
        for k in (1, 2, 3):
            got(wb.at[1 - c, h, k], wc_send.at[h, k - 1], wc_recv.at[h, k - 1])

    def weights(part, h):
        return wb[part, h].reshape(NX * TOK, COLS)

    def project(h):
        await_w(h)
        await_att(h, 0)
        await_att(h, 1)
        for part in (1, 0):
            term = dot(attx[h], weights(part, h))
            pacc[part] = pacc[part] + term if h > 0 else term

    def y_copy(r):
        rows = pl.ds(r * HALF, HALF)
        return ysend.at[rows], yrecv.at[rows], y_send.at[r], y_recv.at[r]

    def project_last():
        h = HEADS - 1
        await_w(h)
        for r in (0, 1):
            rows = pl.ds(r * HALF, HALF)
            await_att(h, r)
            term = pacc[1, rows, :] + dot(attx[h, rows, :], weights(1, h))
            ysend[rows, :] = term.astype(BF16)
            push(*y_copy(r), mate)
        pacc[0] = pacc[0] + dot(attx[h], weights(0, h))

    for h in range(HEADS):
        z_start(h, 1, 0)
        z_start(h, 1, 1)
        q_start(h)
    for h in range(HEADS):
        c_start(h, 0)
    for h in range(HEADS):
        w_start(h)
    for copy in later:
        copy.wait()
    relay(0, 1)
    work(0, 0)
    relay(1, 1)
    work(0, 1)
    relay(0, 2)
    work(1, 0)
    work(1, 1)
    relay(2, 1)
    work(0, 2)
    relay(0, 3)
    work(2, 0)
    work(2, 1)
    relay(1, 2)
    relay(0, 4)
    work(0, 3)
    w_relay(0)
    relay(2, 2)
    work(1, 2)
    work(0, 4)
    finish(0)
    relay(1, 3)
    work(2, 2)
    relay(2, 3)
    relay(1, 4)
    work(1, 3)
    w_relay(1)
    relay(2, 4)
    work(2, 3)
    merge(0, 0)
    merge(0, 1)
    work(1, 4)
    finish(1)
    work(2, 4)
    finish(2)
    w_relay(2)
    merge(1, 0)
    merge(1, 1)
    merge(2, 0)
    merge(2, 1)
    for copy in w_own:
        copy.wait()
    project(0)
    project(1)
    project_last()
    for r in (0, 1):
        rows = pl.ds(r * HALF, HALF)
        _, dst, ssem, rsem = y_copy(r)
        got(dst, ssem, rsem)
        projected = pacc[0, rows, :] + yrecv[rows, :].astype(F32)
        mixed = hidv[rows, :].astype(F32) + gatev[...][None, :] * projected
        out[rows, :] = mixed.astype(BF16)
    for copy in sent:
        copy.wait_send()


def local(hidden_in, queries, fresh_keys, fresh_values, stale_keys, stale_values, out_weight, gate):
    anywhere = pl.BlockSpec(memory_space=pltpu.HBM)
    vmem, dma = pltpu.VMEM, pltpu.SemaphoreType.DMA
    wide = (HEADS, NY * TOK, 128)
    return pl.pallas_call(
        kernel,
        out_shape=jax.ShapeDtypeStruct((TOK, COLS), BF16),
        in_specs=[anywhere] * 8,
        out_specs=pl.BlockSpec(memory_space=pltpu.VMEM),
        scratch_shapes=[
            vmem((HEADS, 5, 2, 4, TOK, 128), BF16),
            vmem((HEADS, NY, TOK, 128), BF16),
            vmem(wide, F32),
            vmem(wide, F32),
            vmem(wide, F32),
            vmem((HEADS, 3, 2 * PART, 128), BF16),
            vmem((HEADS, 3, 2 * PART, 128), BF16),
            vmem((HEADS, TOK, 128), BF16),
            vmem((HEADS, TOK, NX * 128), BF16),
            vmem((2, HEADS, NX, TOK, COLS), BF16),
            vmem((2, TOK, COLS), F32),
            vmem((TOK, COLS), BF16),
            vmem((TOK, COLS), BF16),
            vmem((TOK, COLS), BF16),
            vmem((COLS,), F32),
            dma((HEADS, 6)),
            dma((2,)),
            dma((2, HEADS, 4)),
            dma((2, HEADS, 4)),
            dma((HEADS, 5)),
            dma((HEADS, 5)),
            *[dma((HEADS, 3)) for _ in range(2)],
            *[dma((2, HEADS, 3)) for _ in range(4)],
            *[dma((HEADS, 3)) for _ in range(4)],
            dma((2,)),
            dma((2,)),
        ],
        compiler_params=pltpu.CompilerParams(
            collective_id=0, has_side_effects=True, vmem_limit_bytes=62 * 2**20
        ),
    )(
        hidden_in, queries, fresh_keys, fresh_values, stale_keys, stale_values,
        out_weight.reshape(HEADS, TOK, -1), gate,
    )


def solution(mesh):
    split = P("patch", "tensor")
    return jax.shard_map(
        local,
        mesh=mesh,
        in_specs=(split,) * 6 + (P("tensor", None), P("tensor")),
        out_specs=split,
        check_vma=False,
    )
```
